32 devices in a mesh: grp: 2 (over x), ep: 4 (over y, core), dp: 4 (over z).
Axes of the slice: x: 2, y: 2, z: 4, core: 2. Of those that a mesh axis runs over, the one named last changes fastest.
Arguments:
- hidden_states: bfloat16 [512, 7168], P(('grp', 'ep'), 'dp'), parts along dimension 0, may hold values from -27 to 27
- input_gain: float32 [7168], P('dp'), may hold values from 0.25 to 1.75
- expert_ids: int32 [512, 2], P(('grp', 'ep')), parts along dimension 0, may hold values from 0 to 3, all different within a row; in each aligned block of 64 rows (0 to 63, 64 to 127, ...) at most 64 rows name the same one
- route_scores: float32 [512, 2], P(('grp', 'ep')), parts along dimension 0, may hold values from 0.05 to 1
- w_gate: bfloat16 [4, 7168, 2048], P('ep', None, 'dp'), may hold values from -0.0625 to 0.0625
- w_up: bfloat16 [4, 7168, 2048], P('ep', None, 'dp'), may hold values from -0.0625 to 0.0625
- w_down: bfloat16 [4, 2048, 7168], P('ep', 'dp'), may hold values from -0.1875 to 0.1875
- latent_gain: float32 [7168], P('dp'), may hold values from 0.25 to 1.75
- w_latent: bfloat16 [7168, 576], P('dp'), may hold values from -0.0625 to 0.0625
- kv_gain: float32 [512], replicated, may hold values from 0.25 to 1.75
- seq_lengths: int32 [8, 4], P(('grp', 'ep')), parts along dimension 0, may hold values from 1 to 32, 64 in all within a row
- seq_owners: int32 [8, 4], P(('grp', 'ep')), parts along dimension 0, may hold values from 0 to 3
Outputs:
- mixed_states: bfloat16 [512, 7168], P(('grp', 'ep'), 'dp'), parts along dimension 0
- latent_cache: bfloat16 [8, 4, 64, 576], P(('grp', 'ep'), 'dp'), parts along dimension 0
The draws below stay inside these ranges and needn't reach their ends.
There are 2 independent parts, one for each index of `grp`. The reference program is written for one: setup_inputs(seed, part) draws one part's arguments, and reference() takes and returns one part's arrays. A program takes and returns all parts, laid end to end along the dimension named above; an argument that names none is the same for every part. Nothing has to cross between parts.
Inputs may be any that keep to these rules, and one draw needn't show every extreme that they name: `expert_ids`: each row names 2 different experts; among the 64 rows of one ep block no expert is named more than 64 times, and some block reaches 64. `seq_lengths`: each row sums to 64 and holds one length of exactly 32.
All inputs are finite; a program needn't handle non-finite values.
Results may differ from the reference program's by a relative error of at most 0.015.
Values may be sent and summed in bfloat16 or wider, within the bound.
A program may use at most 128 MiB of HBM per device.

```python
import math
import jax
import jax.numpy as jnp
import numpy as np
from jax import lax

D = 7168
FF = 2048
KVL = 512
ROPE = 64
TOK_EP = 64
SEQS = 4
EXPERTS = 4
TOP = 2
CAP = 64
TOKENS = 256
N_EP = 4
N_DP = 4


def draw_hidden_states(key, part):
    key = jax.random.fold_in(key, 11)
    noise_key, column_key, row_key = jax.random.split(key, 3)
    ramp = 1.0 + 2.0 * jnp.arange(D, dtype=jnp.float32) / D
    column_scale = jnp.exp(jax.random.uniform(column_key, (D,), jnp.float32, math.log(0.3), math.log(1.5))) * ramp
    row_scale = jnp.exp(jax.random.uniform(row_key, (TOKENS, 1), jnp.float32, math.log(0.5), math.log(2.0)))
    values = jnp.clip(jax.random.normal(noise_key, (TOKENS, D), jnp.float32), -3.0, 3.0)
    return (values * column_scale[None, :] * row_scale).astype(jnp.bfloat16)


def plant(result, stream_key, least, largest):
    index_at = [jax.random.randint(jax.random.fold_in(stream_key, axis), (), 0, length) for axis, length in enumerate(result.shape)]
    widest = result.shape.index(max(result.shape))
    neighbour = index_at[:widest] + [(index_at[widest] + 1) % result.shape[widest]] + index_at[widest + 1:]
    return result.at[tuple(index_at)].set(least).at[tuple(neighbour)].set(largest)


def spiked(result, key, source, target, shards_of, factor):
    owner, partner = [(jnp.arange(result.shape[dim]) // (result.shape[dim] // shards_of)).reshape([-1 if axis == dim else 1 for axis in range(result.ndim)]) for dim in (source, target)]
    chosen = jax.random.permutation(key, shards_of)[partner]
    strong = (owner == chosen) | (owner == (partner + shards_of // 2) % shards_of)
    return jnp.where(strong, factor * result, result)


def shard_levels(rng, shape, cuts, low, top_value):
    level = 1.0
    for dim, blocks in cuts:
        draws = jax.random.uniform(jax.random.fold_in(jax.random.fold_in(rng, 6), dim), (blocks,), jnp.float32, low / len(cuts), top_value / len(cuts))
        level = level * jnp.repeat(jnp.exp(draws), shape[dim] // blocks).reshape((-1,) + (1,) * (len(shape) - 1 - dim))
    return level


def split_up(number_of, total, most, slope):
    loads = [(1 << 20) // math.isqrt(grade ** slope) + 1 for grade in range(2, number_of + 1)]
    surplus, given = total - most - (number_of - 1), [1] * (number_of - 1)
    while surplus > 0:
        candidates = [i for i in range(number_of - 1) if given[i] < most]
        whole, remaining = sum([loads[i] for i in candidates]), surplus
        for i in candidates:
            more = min(most - given[i], max(1, remaining * loads[i] // whole), surplus)
            given[i] = given[i] + more
            surplus = surplus - more
    return np.array([most] + given)


def ragged(key, amount, total, limit, slope):
    if amount == 2:
        one = jax.random.randint(key, (), max(1, total - limit), min(limit, total - 1) + 1)
        return jnp.stack([one, total - one])
    sizes = jnp.asarray(split_up(amount, total, limit, slope), jnp.int32)
    twos = (amount - 1) // 2
    giver, receiver = sizes[1:1 + 2 * twos:2], sizes[2:2 + 2 * twos:2]
    margin = jnp.minimum(giver - 1, limit - receiver)
    shifted = jax.random.randint(jax.random.fold_in(key, 1), (twos,), 0, 1 << 20) % (margin + 1)
    sizes = sizes.at[1:1 + 2 * twos:2].set(giver - shifted).at[2:2 + 2 * twos:2].set(receiver + shifted)
    return sizes[jax.random.permutation(jax.random.fold_in(key, 2), amount)]


def deal_out(own_key, own, number, rows, amount, top, bound, lean):
    order = jax.random.permutation(own_key, amount)
    crowded, usual = shares(amount, rows * top, bound, lean, True), shares(amount, rows * top, bound, lean, False)
    places = jnp.arange(amount)

    def named(lengths, turn):
        used = int((lengths > 0).sum())
        fixed = max(1, used // 4)
        moved = fixed + (places - fixed + turn * (used - fixed)) % max(1, amount - fixed)
        return jnp.zeros((amount,), jnp.int32).at[order[jnp.where(places < fixed, places, moved)]].set(jnp.asarray(lengths, jnp.int32))

    lengths = jnp.where(number % 4 == 0, named(crowded, number // 4), named(usual, number - number // 4 - 1))
    mixed = jax.random.permutation(jax.random.fold_in(own, 3), amount)
    giver, receiver = mixed[0:amount // 2 * 2:2], mixed[1:amount // 2 * 2:2]
    room = jnp.minimum(lengths[giver] - 1, bound - lengths[receiver]) // 2
    room = jnp.where((giver == order[0]) | (receiver == order[0]) | (lengths[receiver] == 0), 0, jnp.maximum(room, 0))
    moved = jax.random.randint(jax.random.fold_in(own, 4), (amount // 2,), 0, 1 << 20) % (room + 1)
    lengths = lengths.at[giver].add(-moved).at[receiver].add(moved)
    items = jnp.searchsorted(jnp.cumsum(lengths), jnp.arange(rows * top), side="right").astype(jnp.int32)
    table = items.reshape(top, rows).T
    table = table[jax.random.permutation(jax.random.fold_in(own, 1), rows)]
    turn = jax.random.randint(jax.random.fold_in(own, 2), (rows, 1), 0, top)
    return jnp.take_along_axis(table, (jnp.arange(top)[None, :] + turn) % top, axis=1)


def shares(amount, total, reach, slope, full):
    loads = [(1 << 20) // math.isqrt(rank ** slope) + 1 for rank in range(1, amount + 1)]
    largest = reach if full else min(reach, max(-(-total // amount), total * loads[0] // sum(loads)))
    least = 1 if total - largest >= amount - 1 else 0
    counts, surplus = [largest] + [least] * (amount - 1), total - largest - least * (amount - 1)
    while surplus > 0:
        free = [i for i in range(1, amount) if counts[i] < largest] or [i for i in range(1, amount) if counts[i] < reach]
        mass, budget = sum([loads[i] for i in free]), surplus
        for i in free:
            addition = min(reach - counts[i], max(1, budget * loads[i] // mass), surplus)
            counts[i] = counts[i] + addition
            surplus = surplus - addition
    return np.array(counts)


def normal_values(rng, shape, scale, bound, shards=(), kind=jnp.bfloat16):
    entries = jax.random.normal(rng, shape, jnp.float32) * scale
    if len(shards) > 0:
        entries = shard_levels(rng, shape, shards, -0.22, 0.18) * entries
    return jnp.clip(entries, min=-bound, max=bound).astype(kind)


def noise_with(own_key, shape, scale, bound, cuts, heavy, kind=jnp.bfloat16):
    result = scale * jax.random.normal(own_key, shape, jnp.float32)
    if cuts:
        result = result * shard_levels(own_key, shape, cuts, -0.22, 0.18)
    return jnp.clip(spiked(result, jax.random.fold_in(own_key, 3), *heavy), -bound, bound).astype(kind)


def setup_inputs(seed: int = 0, part: int = 0) -> dict:
    splits = jax.random.split(jax.random.key(seed), 13)
    own_keys = jax.random.split(jax.random.fold_in(splits[12], part), 13)
    hidden_states = draw_hidden_states(jax.random.fold_in(jax.random.fold_in(splits[12], part), 71), part)
    input_gain = jnp.clip(1.0 + 0.15 * jax.random.normal(splits[1], (D,), jnp.float32), 0.25, 1.75)
    expert_ids_keys = jax.random.split(jax.random.fold_in(own_keys[2], 1), TOKENS // TOK_EP)
    expert_ids_turns = jax.random.permutation(jax.random.fold_in(own_keys[2], 3), TOKENS // TOK_EP)
    expert_ids = jax.vmap(lambda own, number: deal_out(jax.random.fold_in(own_keys[2], 2), own, number, TOK_EP, EXPERTS, TOP, CAP, 2))(expert_ids_keys, expert_ids_turns).reshape((TOKENS, TOP))
    route_scores = jnp.clip(jnp.exp(math.log(1.0) - 2.9957323 * jax.random.uniform(own_keys[3], (TOKENS, TOP), jnp.float32) ** shard_levels(own_keys[3], (TOKENS, TOP), ((0, 4),), -0.2, 0.2)), 0.05, 1.0)
    w_gate = normal_values(splits[4], (EXPERTS, D, FF), D ** -0.5, 0.0625, ((0, 4), (2, 4)))
    w_up = normal_values(splits[5], (EXPERTS, D, FF), D ** -0.5, 0.0625, ((0, 4), (2, 4)))
    w_down = noise_with(splits[6], (EXPERTS, FF, D), FF ** -0.5, 0.1875, ((0, 4), (1, 4)), (1, 2, 4, 2.0))
    latent_gain = jnp.clip(1.0 + 0.15 * jax.random.normal(splits[7], (D,), jnp.float32), 0.25, 1.75)
    w_latent = normal_values(splits[8], (D, KVL + ROPE), D ** -0.5, 0.0625, ((0, 4),))
    kv_gain = jnp.clip(1.0 + 0.15 * jax.random.normal(splits[9], (KVL,), jnp.float32), 0.25, 1.75)
    seq_lengths = jax.vmap(lambda own: ragged(own, SEQS, TOK_EP, TOK_EP // 2, 2))(jax.random.split(own_keys[10], N_EP)).reshape((N_EP, SEQS)).astype(jnp.int32)
    seq_owners = plant(jax.random.randint(own_keys[11], (N_EP, SEQS), 0, N_DP), jax.random.fold_in(own_keys[11], 1), 0, N_DP - 1).astype(jnp.int32)
    return dict(hidden_states=hidden_states, input_gain=input_gain, expert_ids=expert_ids, route_scores=route_scores, w_gate=w_gate, w_up=w_up, w_down=w_down, latent_gain=latent_gain, w_latent=w_latent, kv_gain=kv_gain, seq_lengths=seq_lengths, seq_owners=seq_owners)


EPSILON = 1e-06
ROUTE_SCALE = 2.5

def slot_table(block_ids, expert_count):
    flat_ids = block_ids.reshape(-1)
    one_hot = (flat_ids[:, None] == jnp.arange(expert_count, dtype=jnp.int32)[None, :]).astype(jnp.int32)
    earlier = jnp.cumsum(one_hot, axis=0) - one_hot
    return (flat_ids, lax.optimization_barrier(jnp.sum(earlier * one_hot, axis=1)).astype(jnp.int32))

def sequence_info(token_index, seq_lengths, seq_owners):
    seq_ends = jnp.cumsum(seq_lengths).astype(jnp.int32)
    seq_number = lax.optimization_barrier(jnp.sum((token_index[:, None] >= seq_ends[None, :]).astype(jnp.int32), axis=1))
    member = (seq_number[:, None] == jnp.arange(seq_lengths.shape[0], dtype=jnp.int32)[None, :]).astype(jnp.int32)
    seq_starts = seq_ends - seq_lengths
    positions = token_index - lax.optimization_barrier(jnp.sum(member * seq_starts[None, :], axis=1))
    owner_of = lax.optimization_barrier(jnp.sum(member * seq_owners[None, :], axis=1))
    return (positions.astype(jnp.int32), owner_of.astype(jnp.int32))

def rope_rotate(rope_keys, positions, rope_width):
    half_width = rope_width // 2
    frequency = jnp.exp(jnp.arange(half_width, dtype=jnp.float32) * (-2.0 * math.log(10000.0) / rope_width))
    angles = positions.astype(jnp.float32)[:, None] * frequency[None, :]
    cosine = jnp.cos(angles)
    sine_part = jnp.sin(angles)
    first_half = rope_keys[:, :half_width]
    second_half = rope_keys[:, half_width:]
    return jnp.concatenate([first_half * cosine - second_half * sine_part, second_half * cosine + first_half * sine_part], axis=1)

def finish_latent(latent_sum, positions, kv_gain):
    kv_width = kv_gain.shape[0]
    compressed = latent_sum[:, :kv_width]
    mean_square = lax.optimization_barrier(jnp.mean(compressed * compressed, axis=1, keepdims=True))
    normed_kv = compressed * lax.rsqrt(mean_square + EPSILON) * kv_gain[None, :]
    rotated = rope_rotate(latent_sum[:, kv_width:], positions, latent_sum.shape[1] - kv_width)
    return jnp.concatenate([normed_kv, rotated], axis=1).astype(jnp.bfloat16)

def owner_rows(finished, owner_of, owner_index):
    owned_mask = (owner_of == owner_index).astype(jnp.int32)
    row_rank = jnp.cumsum(owned_mask) - owned_mask
    picker = ((row_rank[None, :] == jnp.arange(finished.shape[0], dtype=jnp.int32)[:, None]) & (owned_mask[None, :] == 1)).astype(jnp.bfloat16)
    return jnp.dot(picker, finished, preferred_element_type=jnp.float32).astype(jnp.bfloat16)

def reference(hidden_states, input_gain, expert_ids, route_scores, w_gate, w_up, w_down, latent_gain, w_latent, kv_gain, seq_lengths, seq_owners):
    states = hidden_states.astype(jnp.float32)
    mean_square = lax.optimization_barrier(jnp.mean(states * states, axis=1, keepdims=True))
    normed = (states * lax.rsqrt(mean_square + EPSILON) * input_gain[None, :]).astype(jnp.bfloat16)
    route_weights = ROUTE_SCALE * route_scores / lax.optimization_barrier(jnp.sum(route_scores, axis=1, keepdims=True))
    block_ids = expert_ids.reshape(N_EP, TOK_EP * TOP)
    flat_ids, slot_index = jax.vmap(lambda ids_block: slot_table(ids_block, EXPERTS))(block_ids)
    block_number = jnp.arange(N_EP, dtype=jnp.int32)[:, None]
    row_index = slot_index * N_EP + block_number
    token_of = jnp.repeat(jnp.arange(TOKENS, dtype=jnp.int32), TOP)
    dispatched = jnp.zeros((EXPERTS, CAP * N_EP, D), jnp.bfloat16)
    dispatched = dispatched.at[flat_ids.reshape(-1), row_index.reshape(-1)].set(normed[token_of])
    shard_width = FF // N_DP

    def run_expert(operands):
        expert_rows, gate_matrix, up_matrix, down_matrix = operands
        gate_sum = jnp.dot(expert_rows, gate_matrix, preferred_element_type=jnp.float32)
        up_sum = jnp.dot(expert_rows, up_matrix, preferred_element_type=jnp.float32)
        hidden_units = (jax.nn.silu(gate_sum) * up_sum).astype(jnp.bfloat16)
        running_sum = jnp.zeros((expert_rows.shape[0], D), jnp.float32)
        for shard_index in range(N_DP):
            lower = shard_index * shard_width
            part_sum = jnp.dot(hidden_units[:, lower:lower + shard_width], down_matrix[lower:lower + shard_width], preferred_element_type=jnp.float32).astype(jnp.bfloat16)
            running_sum = running_sum + lax.optimization_barrier(part_sum).astype(jnp.float32)
        return running_sum.astype(jnp.bfloat16)
    expert_out = lax.map(run_expert, (dispatched, w_gate, w_up, w_down))
    picked = expert_out[flat_ids.reshape(-1), row_index.reshape(-1)].reshape(TOKENS, TOP, D).astype(jnp.float32)
    mixed_states = (states + lax.optimization_barrier(jnp.sum(route_weights[:, :, None] * picked, axis=1))).astype(jnp.bfloat16)
    layer_out = mixed_states.astype(jnp.float32)
    out_square = lax.optimization_barrier(jnp.mean(layer_out * layer_out, axis=1, keepdims=True))
    normed_out = (layer_out * lax.rsqrt(out_square + EPSILON) * latent_gain[None, :]).astype(jnp.bfloat16)
    latent = jnp.dot(normed_out, w_latent, preferred_element_type=jnp.float32)
    local_index = jnp.arange(TOK_EP, dtype=jnp.int32)
    positions, owner_blocks = jax.vmap(lambda lengths_row, owners_row: sequence_info(local_index, lengths_row, owners_row))(seq_lengths, seq_owners)
    finished = finish_latent(latent, positions.reshape(TOKENS), kv_gain)
    finished_blocks = finished.reshape(N_EP, TOK_EP, KVL + ROPE)
    owner_list = jnp.arange(N_DP, dtype=jnp.int32)

    def block_cache(finished_block, owner_block):
        return jax.vmap(lambda owner_index: owner_rows(finished_block, owner_block, owner_index))(owner_list)
    latent_cache = jax.vmap(block_cache)(finished_blocks, owner_blocks)
    return (mixed_states, latent_cache)
```

```python
import functools
import math

import jax
import jax.numpy as jnp
from jax import lax
from jax.experimental import pallas as pl
from jax.experimental.pallas import tpu as pltpu
from jax.sharding import PartitionSpec as P

EPSILON = 1e-06
ROUTE_SCALE = 2.5
LANES = 128
F32 = jnp.float32
BF16 = jnp.bfloat16


def flipped(index, k, count):
    out = index
    bit = 1
    while bit < count:
        out = out + bit * ((k // bit) % 2) * (1 - 2 * ((index // bit) % 2))
        bit *= 2
    return out


def loop(lower, upper, body):
    def step(i, carry):
        body(i)
        return carry

    lax.fori_loop(lower, upper, step, 0)


def split_f32(value):
    high = value.astype(BF16).astype(F32)
    return high, value - high


def kernel(
    n_ep,
    n_dp,
    states_ref,
    gain_ref,
    ids_ref,
    scores_ref,
    wg_hbm,
    wu_hbm,
    wd_hbm,
    lgain_ref,
    wl_hbm,
    kvgain_ref,
    lengths_ref,
    owners_ref,
    mixed_ref,
    cache_ref,
    xbuf,
    wg,
    wu,
    wd,
    wl,
    acc_g,
    acc_u,
    hid,
    crecv,
    yrecv,
    zrecv,
    latbuf,
    latrecv,
    w_sem,
    g_recv,
    gz_send,
    gy_send,
    gc_send,
    rc_send,
    rc_recv,
    ry_send,
    ry_recv,
    rz_send,
    rz_recv,
    l_send,
    l_recv,
):
    tok, fs = states_ref.shape
    top = ids_ref.shape[1]
    rows = n_ep * tok
    width = fs * n_dp
    n_y = n_ep // 2
    seqs = lengths_ref.shape[1]
    kvl = kvgain_ref.shape[1]
    lat_width = wl.shape[1]
    me = lax.axis_index("ep")
    z = lax.axis_index("dp")
    y = me // 2
    c = me % 2
    peer = y * 2 + (1 - c)

    def rem(src, dst, send, recv, **where):
        return pltpu.make_async_remote_copy(
            src_ref=src,
            dst_ref=dst,
            send_sem=send,
            recv_sem=recv,
            device_id=where,
            device_id_type=pl.DeviceIdType.MESH,
        )

    weight_copies = [
        pltpu.make_async_copy(wg_hbm.at[0], wg, w_sem.at[0]),
        pltpu.make_async_copy(wu_hbm.at[0], wu, w_sem.at[1]),
        pltpu.make_async_copy(wd_hbm.at[0], wd, w_sem.at[2]),
        pltpu.make_async_copy(wl_hbm, wl, w_sem.at[3]),
    ]

    barrier = pltpu.get_barrier_semaphore()
    for k in range(1, n_dp):
        pl.semaphore_signal(
            barrier, inc=1, device_id={"dp": flipped(z, k, n_dp)},
            device_id_type=pl.DeviceIdType.MESH,
        )
    for k in range(1, n_y):
        pl.semaphore_signal(
            barrier, inc=1, device_id={"ep": ((y + k) % n_y) * 2 + c},
            device_id_type=pl.DeviceIdType.MESH,
        )
    pl.semaphore_signal(
        barrier, inc=1, device_id={"ep": peer}, device_id_type=pl.DeviceIdType.MESH
    )

    states = states_ref[...].astype(F32)
    xbuf[z, me, :, pl.ds(0, fs)] = (states * gain_ref[...]).astype(BF16)
    square = jnp.sum(states * states, axis=1, keepdims=True)
    scores = scores_ref[...]
    weights = ROUTE_SCALE * scores / jnp.sum(scores, axis=1, keepdims=True)
    lane = lax.broadcasted_iota(jnp.int32, (tok, LANES), 1)
    half = LANES // 2
    folded = lane % half
    extra = jnp.where(folded == n_ep, square, 0.0)
    for k in range(top):
        extra += jnp.where(folded == ids_ref[:, k : k + 1], weights[:, k : k + 1], 0.0)
    high, low = split_f32(extra)
    xbuf[z, me, :, pl.ds(fs, LANES)] = jnp.where(lane < half, high, low).astype(BF16)

    pl.semaphore_wait(barrier, n_dp - 1 + n_y - 1 + 1)

    def gather_z(k):
        to = flipped(z, k, n_dp)
        return rem(xbuf.at[z, me], xbuf.at[z, me], gz_send.at[k], g_recv.at[z, me], dp=to)

    def gather_y(s, j):
        to = ((y + j) % n_y) * 2 + c
        return rem(xbuf.at[s, me], xbuf.at[s, me], gy_send.at[s, j], g_recv.at[s, me], ep=to)

    def gather_c(s, yy):
        b = yy * 2 + c
        return rem(xbuf.at[s, b], xbuf.at[s, b], gc_send.at[s, yy], g_recv.at[s, b], ep=peer)

    def gather_wait(s, b):
        rem(xbuf.at[s, b], xbuf.at[s, b], g_recv.at[s, b], g_recv.at[s, b], ep=peer).wait_recv()

    loop(1, n_dp, lambda k: gather_z(k).start())

    acc_g[...] = jnp.zeros_like(acc_g)
    acc_u[...] = jnp.zeros_like(acc_u)

    def gather_step(i):
        @pl.when(i < n_dp)
        def _():
            s = flipped(z, i, n_dp)

            @pl.when(i > 0)
            def _():
                gather_wait(s, me)

            loop(1, n_y, lambda j: gather_y(s, j).start())
            gather_c(s, y).start()

        @pl.when(i == 0)
        def _():
            for copy in weight_copies:
                copy.start()

        @pl.when((i >= 1) & (i <= n_dp))
        def _():
            s = flipped(z, i - 1, n_dp)

            def forward(j):
                yy = (y + j) % n_y
                gather_wait(s, yy * 2 + c)
                gather_c(s, yy).start()

            loop(1, n_y, forward)

        @pl.when(i == 2)
        def _():
            weight_copies[0].wait()
            weight_copies[1].wait()

        @pl.when(i >= 2)
        def _():
            s = flipped(z, i - 2, n_dp)
            loop(0, n_y, lambda yy: gather_wait(s, yy * 2 + (1 - c)))
            slab = xbuf[s, :, :, pl.ds(0, fs)].reshape(rows, fs)
            depth = pl.ds(pl.multiple_of(s * fs, LANES), fs)
            acc_g[...] += jnp.dot(slab, wg[depth, :], preferred_element_type=F32)
            acc_u[...] += jnp.dot(slab, wu[depth, :], preferred_element_type=F32)

    loop(0, n_dp + 2, gather_step)

    side = jnp.zeros((rows, LANES), F32)
    wide_lane = lax.broadcasted_iota(jnp.int32, (rows, LANES), 1) % half
    for s in range(n_dp):
        part = xbuf[s, :, :, pl.ds(fs, LANES)].reshape(rows, LANES).astype(F32)
        if s == 0:
            route = jnp.sum(jnp.where(wide_lane == me, part, 0.0), axis=1, keepdims=True)
        side += part
    total = jnp.sum(jnp.where(wide_lane == n_ep, side, 0.0), axis=1, keepdims=True)
    scale = lax.rsqrt(total / width + EPSILON)
    gate = acc_g[...] * scale
    up = acc_u[...] * scale
    hid[...] = (route * (gate / (1.0 + jnp.exp(-gate)) * up)).astype(BF16)

    loop(1, n_dp, lambda k: gather_z(k).wait_send())

    def gather_drain(s):
        loop(1, n_y, lambda j: gather_y(s, j).wait_send())
        loop(0, n_y, lambda yy: gather_c(s, yy).wait_send())

    loop(0, n_dp, gather_drain)
    weight_copies[2].wait()

    def slot(s, b):
        return xbuf.at[s, b, :, pl.ds(0, fs)]

    def reduce_c(s, yy):
        return rem(
            slot(s, yy * 2 + (1 - c)), crecv.at[s, yy], rc_send.at[s, yy], rc_recv.at[s, yy],
            ep=peer,
        )

    def reduce_y(s, j):
        to = (y + j) % n_y
        return rem(
            slot(s, to * 2 + c), yrecv.at[s, j], ry_send.at[s, j], ry_recv.at[s, j],
            ep=to * 2 + c,
        )

    def reduce_z(k):
        to = flipped(z, k, n_dp)
        return rem(slot(to, me), zrecv.at[k], rz_send.at[k], rz_recv.at[k], dp=to)

    tile = 256 if fs % 256 == 0 else LANES

    def reduce_step(i):
        @pl.when(i < n_dp)
        def _():
            s = flipped(z, n_dp - 1 - i, n_dp)
            for n in range(fs // tile):
                cols = pl.ds(pl.multiple_of(s * fs + n * tile, LANES), tile)
                out = jnp.dot(hid[...], wd[:, cols], preferred_element_type=F32)
                xbuf[s, :, :, pl.ds(n * tile, tile)] = out.astype(BF16).reshape(n_ep, tok, tile)
            loop(1, n_y + 1, lambda j: reduce_c(s, (y + j) % n_y).start())

        @pl.when((i >= 1) & (i <= n_dp))
        def _():
            s = flipped(z, n_dp - i, n_dp)

            def add(j):
                yy = (y + j) % n_y
                b = yy * 2 + c
                reduce_c(s, yy).wait_recv()
                xbuf[s, b, :, pl.ds(0, fs)] = (
                    xbuf[s, b, :, pl.ds(0, fs)].astype(F32) + crecv[s, yy].astype(F32)
                ).astype(BF16)

                @pl.when(j < n_y)
                def _():
                    reduce_y(s, j).start()

            loop(1, n_y + 1, add)

        @pl.when(i >= 2)
        def _():
            k = n_dp + 1 - i
            s = flipped(z, k, n_dp)

            def add(j):
                reduce_y(s, j).wait_recv()
                xbuf[s, me, :, pl.ds(0, fs)] = (
                    xbuf[s, me, :, pl.ds(0, fs)].astype(F32) + yrecv[s, j].astype(F32)
                ).astype(BF16)

            loop(1, n_y, add)

            @pl.when(k > 0)
            def _():
                reduce_z(k).start()

    loop(0, n_dp + 2, reduce_step)

    routed = xbuf[z, me, :, pl.ds(0, fs)].astype(F32)
    for k in range(n_dp - 1, 0, -1):
        reduce_z(k).wait_recv()
        routed += zrecv[k].astype(F32)
    mixed = (states_ref[...].astype(F32) + routed).astype(BF16)
    mixed_ref[...] = mixed

    layer = mixed.astype(F32)
    gained = (layer * lgain_ref[...]).astype(BF16)
    out_square = jnp.sum(layer * layer, axis=1, keepdims=True)
    weight_copies[3].wait()
    pad_width = latbuf.shape[1]
    latbuf[:, pl.ds(0, lat_width)] = jnp.dot(
        gained, wl[...], preferred_element_type=F32
    ).astype(BF16)
    high, low = split_f32(out_square)
    spare = lax.broadcasted_iota(jnp.int32, (tok, pad_width - lat_width), 1)
    latbuf[:, pl.ds(lat_width, pad_width - lat_width)] = jnp.where(
        spare == 0, high, jnp.where(spare == 1, low, 0.0)
    ).astype(BF16)

    def latent(k):
        return rem(
            latbuf, latrecv.at[k], l_send.at[k], l_recv.at[k], dp=flipped(z, k, n_dp)
        )

    for k in range(1, n_dp):
        latent(k).start()

    rope = lat_width - kvl
    turn = rope // 2
    tail = pad_width - kvl
    token = lax.broadcasted_iota(jnp.int32, (tok, tail), 0)
    across = lax.broadcasted_iota(jnp.int32, (tok, tok), 1)
    begin = jnp.int32(0)
    position = token
    owner = jnp.zeros((tok, tok), jnp.int32)
    for j in range(seqs):
        end = begin + lengths_ref[0, j]
        position = jnp.where((token >= begin) & (token < end), token - begin, position)
        owner = jnp.where((across >= begin) & (across < end), owners_ref[0, j], owner)
        begin = end
    column = lax.broadcasted_iota(jnp.int32, (tok, tail), 1)
    frequency = jnp.exp((column % turn).astype(F32) * (-2.0 * math.log(10000.0) / rope))
    angle = position.astype(F32) * frequency
    cosine = jnp.cos(angle)
    sine = jnp.sin(angle)
    sine = jnp.where(column < turn, -sine, sine)
    down = lax.broadcasted_iota(jnp.int32, (tok, tok), 0)
    mine = (owner == z).astype(F32)
    rank = jnp.dot(mine, (down < across).astype(F32), preferred_element_type=F32)
    picker = jnp.where((rank == down.astype(F32)) & (owner == z), 1.0, 0.0).astype(BF16)

    summed = latbuf[...].astype(F32)
    for k in range(1, n_dp):
        latent(k).wait_recv()
        summed += latrecv[k].astype(F32)
    end_part = summed[:, kvl:]
    in_square = jnp.where(
        (column == rope) | (column == rope + 1), end_part, 0.0
    )
    out_scale = lax.rsqrt(jnp.sum(in_square, axis=1, keepdims=True) / width + EPSILON)
    compressed = summed[:, :kvl] * out_scale
    mean_square = jnp.mean(compressed * compressed, axis=1, keepdims=True)
    normed = compressed * lax.rsqrt(mean_square + EPSILON) * kvgain_ref[...]
    keys = end_part * out_scale
    swapped = jnp.where(
        column < turn, pltpu.roll(keys, tail - turn, 1), pltpu.roll(keys, turn, 1)
    )
    rotated = keys * cosine + swapped * sine
    cache_ref[0, 0, :, pl.ds(0, kvl)] = jnp.dot(
        picker, normed.astype(BF16), preferred_element_type=F32
    ).astype(BF16)
    picked = jnp.dot(picker, rotated.astype(BF16), preferred_element_type=F32).astype(BF16)
    cache_ref[0, 0, :, pl.ds(kvl, rope)] = picked[:, :rope]

    for k in range(1, n_dp):
        latent(k).wait_send()
        reduce_z(k).wait_send()

    def reduce_drain(s):
        loop(1, n_y, lambda j: reduce_y(s, j).wait_send())
        loop(0, n_y, lambda yy: reduce_c(s, yy).wait_send())

    loop(0, n_dp, reduce_drain)


def on_device(
    hidden_states,
    input_gain,
    expert_ids,
    route_scores,
    w_gate,
    w_up,
    w_down,
    latent_gain,
    w_latent,
    kv_gain,
    seq_lengths,
    seq_owners,
):
    tok, fs = hidden_states.shape
    n_ep = lax.axis_size("ep")
    n_dp = lax.axis_size("dp")
    n_y = n_ep // 2
    rows = n_ep * tok
    width, units = w_gate.shape[1:]
    lat_width = w_latent.shape[1]
    kvl = kv_gain.shape[0]
    pad_width = kvl + LANES
    vmem = pl.BlockSpec(memory_space=pltpu.VMEM)
    hbm = pl.BlockSpec(memory_space=pl.ANY)
    smem = pl.BlockSpec(memory_space=pltpu.SMEM)
    dma = pltpu.SemaphoreType.DMA
    return pl.pallas_call(
        functools.partial(kernel, n_ep, n_dp),
        out_shape=(
            jax.ShapeDtypeStruct((tok, fs), BF16),
            jax.ShapeDtypeStruct((1, 1, tok, lat_width), BF16),
        ),
        in_specs=[vmem, vmem, vmem, vmem, hbm, hbm, hbm, vmem, hbm, vmem, smem, smem],
        out_specs=(vmem, vmem),
        scratch_shapes=[
            pltpu.VMEM((n_dp, n_ep, tok, fs + LANES), BF16),
            pltpu.VMEM((width, units), BF16),
            pltpu.VMEM((width, units), BF16),
            pltpu.VMEM((units, width), BF16),
            pltpu.VMEM((fs, lat_width), BF16),
            pltpu.VMEM((rows, units), F32),
            pltpu.VMEM((rows, units), F32),
            pltpu.VMEM((rows, units), BF16),
            pltpu.VMEM((n_dp, n_y, tok, fs), BF16),
            pltpu.VMEM((n_dp, n_y, tok, fs), BF16),
            pltpu.VMEM((n_dp, tok, fs), BF16),
            pltpu.VMEM((tok, pad_width), BF16),
            pltpu.VMEM((n_dp, tok, pad_width), BF16),
            dma((4,)),
            dma((n_dp, n_ep)),
            dma((n_dp,)),
            dma((n_dp, n_y)),
            dma((n_dp, n_y)),
            dma((n_dp, n_y)),
            dma((n_dp, n_y)),
            dma((n_dp, n_y)),
            dma((n_dp, n_y)),
            dma((n_dp,)),
            dma((n_dp,)),
            dma((n_dp,)),
            dma((n_dp,)),
        ],
        compiler_params=pltpu.CompilerParams(
            collective_id=0, has_side_effects=True, vmem_limit_bytes=60 * 2**20
        ),
    )(
        hidden_states,
        input_gain[None, :],
        expert_ids,
        route_scores,
        w_gate,
        w_up,
        w_down,
        latent_gain[None, :],
        w_latent,
        kv_gain[None, :],
        seq_lengths,
        seq_owners,
    )


def solution(mesh):
    return jax.shard_map(
        on_device,
        mesh=mesh,
        in_specs=(
            P(("grp", "ep"), "dp"),
            P("dp"),
            P(("grp", "ep"), None),
            P(("grp", "ep"), None),
            P("ep", None, "dp"),
            P("ep", None, "dp"),
            P("ep", "dp", None),
            P("dp"),
            P("dp", None),
            P(),
            P(("grp", "ep"), None),
            P(("grp", "ep"), None),
        ),
        out_specs=(P(("grp", "ep"), "dp"), P(("grp", "ep"), "dp", None, None)),
        check_vma=False,
    )
```

```python
import functools
import math

import jax
import jax.numpy as jnp
from jax import lax
from jax.experimental import pallas as pl
from jax.experimental.pallas import tpu as pltpu
from jax.sharding import PartitionSpec as P

EPSILON = 1e-06
ROUTE_SCALE = 2.5
LANES = 128
PARTS = 2
F32 = jnp.float32
BF16 = jnp.bfloat16


def flipped(index, k, count):
    out = index
    bit = 1
    while bit < count:
        out = out + bit * ((k // bit) % 2) * (1 - 2 * ((index // bit) % 2))
        bit *= 2
    return out


def loop(lower, upper, body):
    def step(i, carry):
        body(i)
        return carry

    lax.fori_loop(lower, upper, step, 0)


def split_f32(value):
    high = value.astype(BF16).astype(F32)
    return high, value - high


def kernel(
    n_ep,
    n_dp,
    states_ref,
    gain_ref,
    ids_ref,
    scores_ref,
    wg_hbm,
    wu_hbm,
    wd_hbm,
    lgain_ref,
    wl_hbm,
    kvgain_ref,
    lengths_ref,
    owners_ref,
    mixed_ref,
    cache_ref,
    xbuf,
    wg,
    wu,
    wd,
    wl,
    acc_g,
    acc_u,
    hid,
    crecv,
    yrecv,
    zrecv,
    latbuf,
    latrecv,
    w_sem,
    g_recv,
    gz_send,
    gy_send,
    gc_send,
    rc_send,
    rc_recv,
    ry_send,
    ry_recv,
    rz_send,
    rz_recv,
    l_send,
    l_recv,
):
    tok, fs = states_ref.shape
    top = ids_ref.shape[0]
    rows = n_ep * tok
    width = fs * n_dp
    n_y = n_ep // 2
    seqs = lengths_ref.shape[1]
    kvl = kvgain_ref.shape[0]
    lat_width = wl.shape[0]
    me = lax.axis_index("ep")
    z = lax.axis_index("dp")
    y = me // 2
    c = me % 2
    peer = y * 2 + (1 - c)
    part = tok // PARTS

    def rem(src, dst, send, recv, **where):
        return pltpu.make_async_remote_copy(
            src_ref=src,
            dst_ref=dst,
            send_sem=send,
            recv_sem=recv,
            device_id=where,
            device_id_type=pl.DeviceIdType.MESH,
        )

    weight_copies = [
        pltpu.make_async_copy(wg_hbm.at[0], wg, w_sem.at[0]),
        pltpu.make_async_copy(wu_hbm.at[0], wu, w_sem.at[1]),
        pltpu.make_async_copy(wd_hbm.at[0], wd, w_sem.at[2]),
        pltpu.make_async_copy(wl_hbm, wl, w_sem.at[3]),
    ]

    barrier = pltpu.get_barrier_semaphore()
    for k in range(1, n_dp):
        pl.semaphore_signal(
            barrier, inc=1, device_id={"dp": flipped(z, k, n_dp)},
            device_id_type=pl.DeviceIdType.MESH,
        )
    for k in range(1, n_y):
        pl.semaphore_signal(
            barrier, inc=1, device_id={"ep": ((y + k) % n_y) * 2 + c},
            device_id_type=pl.DeviceIdType.MESH,
        )
    pl.semaphore_signal(
        barrier, inc=1, device_id={"ep": peer}, device_id_type=pl.DeviceIdType.MESH
    )

    states = states_ref[...].astype(F32)
    xbuf[z, me, :, pl.ds(0, fs)] = (states * gain_ref[...][None, :]).astype(BF16)
    square = jnp.sum(states * states, axis=1, keepdims=True)
    scores = scores_ref[...]
    weights = ROUTE_SCALE * scores / jnp.sum(scores, axis=0, keepdims=True)
    half = LANES // 2
    across = lax.broadcasted_iota(jnp.int32, (LANES, tok), 0) % half
    named = jnp.zeros((LANES, tok), F32)
    for k in range(top):
        named += jnp.where(across == ids_ref[k : k + 1, :], weights[k : k + 1, :], 0.0)
    lane = lax.broadcasted_iota(jnp.int32, (tok, LANES), 1)
    extra = jnp.where(lane % half == n_ep, square, named.T)
    high, low = split_f32(extra)
    xbuf[z, me, :, pl.ds(fs, LANES)] = jnp.where(lane < half, high, low).astype(BF16)

    pl.semaphore_wait(barrier, n_dp - 1 + n_y - 1 + 1)

    def block(s, b, h):
        return xbuf.at[s, b, pl.ds(pl.multiple_of(h * part, part), part)]

    def gather_z(s, h, way):
        return rem(
            block(s, me, h), block(s, me, h), gz_send.at[s, h, way], g_recv.at[s, me, h],
            dp=(z + 2 * way - 1 + n_dp) % n_dp,
        )

    def relay(s, h, act):
        @pl.when((s <= z) & (z + 1 < n_dp))
        def _():
            act(gather_z(s, h, 1))

        @pl.when((s >= z) & (z > 0))
        def _():
            act(gather_z(s, h, 0))

    def gather_y(s, j, h):
        to = ((y + j) % n_y) * 2 + c
        return rem(
            block(s, me, h), block(s, me, h), gy_send.at[s, j, h], g_recv.at[s, me, h], ep=to
        )

    def gather_c(s, yy, h):
        b = yy * 2 + c
        return rem(
            block(s, b, h), block(s, b, h), gc_send.at[s, yy, h], g_recv.at[s, b, h], ep=peer
        )

    def gather_wait(s, b, h):
        rem(
            block(s, b, h), block(s, b, h), g_recv.at[s, b, h], g_recv.at[s, b, h], ep=peer
        ).wait_recv()

    def at_distance(i, body):
        @pl.when(z - i >= 0)
        def _():
            body(z - i)

        @pl.when((i > 0) & (z + i < n_dp))
        def _():
            body(z + i)

    acc_g[...] = jnp.zeros_like(acc_g)
    acc_u[...] = jnp.zeros_like(acc_u)

    def spread(i):
        def body(s):
            def send(h):
                @pl.when(i > 0)
                def _():
                    gather_wait(s, me, h)

                relay(s, h, lambda copy: copy.start())
                loop(1, n_y, lambda j: gather_y(s, j, h).start())
                gather_c(s, y, h).start()

            loop(0, PARTS, send)

        at_distance(i, body)

    def across_core(s):
        def forward(j):
            yy = (y + j) % n_y

            def send(h):
                gather_wait(s, yy * 2 + c, h)
                gather_c(s, yy, h).start()

            loop(0, PARTS, send)

        loop(1, n_y, forward)

    def multiply(s):
        def arrive(yy):
            loop(0, PARTS, lambda h: gather_wait(s, yy * 2 + (1 - c), h))

        loop(0, n_y, arrive)
        slab = xbuf[s, :, :, pl.ds(0, fs)].reshape(rows, fs)
        depth = pl.ds(pl.multiple_of(s * fs, LANES), fs)
        acc_g[...] += jnp.dot(slab, wg[depth, :], preferred_element_type=F32)
        acc_u[...] += jnp.dot(slab, wu[depth, :], preferred_element_type=F32)

    def gather_step(i):
        @pl.when(i < n_dp)
        def _():
            spread(i)

        @pl.when(i == 0)
        def _():
            for copy in weight_copies:
                copy.start()

        @pl.when((i >= 1) & (i <= n_dp))
        def _():
            at_distance(i - 1, across_core)

        @pl.when(i == 2)
        def _():
            weight_copies[0].wait()
            weight_copies[1].wait()

        @pl.when(i >= 2)
        def _():
            at_distance(i - 2, multiply)

    loop(0, n_dp + 2, gather_step)

    side = jnp.zeros((rows, LANES), F32)
    wide_lane = lax.broadcasted_iota(jnp.int32, (rows, LANES), 1) % half
    for s in range(n_dp):
        lanes = xbuf[s, :, :, pl.ds(fs, LANES)].reshape(rows, LANES).astype(F32)
        if s == 0:
            route = jnp.sum(jnp.where(wide_lane == me, lanes, 0.0), axis=1, keepdims=True)
        side += lanes
    total = jnp.sum(jnp.where(wide_lane == n_ep, side, 0.0), axis=1, keepdims=True)
    scale = lax.rsqrt(total / width + EPSILON)
    gate = acc_g[...] * scale
    up = acc_u[...] * scale
    hid[...] = (route * (gate / (1.0 + jnp.exp(-gate)) * up)).astype(BF16)

    def gather_drain(s):
        def drain(h):
            relay(s, h, lambda copy: copy.wait_send())
            loop(1, n_y, lambda j: gather_y(s, j, h).wait_send())
            loop(0, n_y, lambda yy: gather_c(s, yy, h).wait_send())

        loop(0, PARTS, drain)

    loop(0, n_dp, gather_drain)
    weight_copies[2].wait()

    def slot(s, b, h):
        return xbuf.at[s, b, pl.ds(pl.multiple_of(h * part, part), part), pl.ds(0, fs)]

    def half_of(buf, s, j, h):
        return buf.at[s, j, pl.ds(pl.multiple_of(h * part, part), part)]

    def reduce_c(s, yy, h):
        return rem(
            slot(s, yy * 2 + (1 - c), h), half_of(crecv, s, yy, h),
            rc_send.at[s, yy, h], rc_recv.at[s, yy, h], ep=peer,
        )

    def reduce_y(s, j, h):
        to = (y + j) % n_y
        return rem(
            slot(s, to * 2 + c, h), half_of(yrecv, s, j, h),
            ry_send.at[s, j, h], ry_recv.at[s, j, h], ep=to * 2 + c,
        )

    def reduce_z(s, h, way):
        return rem(
            slot(s, me, h), half_of(zrecv, way, s, h),
            rz_send.at[s, h], rz_recv.at[way, s, h], dp=(z + 2 * way - 1 + n_dp) % n_dp,
        )

    def add_into(s, b, h, arrived):
        here = slot(s, b, h)
        here[...] = (here[...].astype(F32) + arrived[...].astype(F32)).astype(BF16)

    def order(q):
        ahead = n_dp - 1 - z
        low = jnp.where(q < ahead, n_dp - 1 - q, q - ahead)
        high = jnp.where(q < z, q, n_dp - 1 - (q - z))
        return jnp.where(q == n_dp - 1, z, jnp.where(2 * z < n_dp, low, high))

    tile = 256 if fs % 256 == 0 else LANES

    def produce_step(i):
        @pl.when(i < n_dp)
        def _():
            s = order(i)
            for n in range(fs // tile):
                cols = pl.ds(pl.multiple_of(s * fs + n * tile, LANES), tile)
                out = jnp.dot(hid[...], wd[:, cols], preferred_element_type=F32)
                xbuf[s, :, :, pl.ds(n * tile, tile)] = out.astype(BF16).reshape(n_ep, tok, tile)

            def send(j):
                loop(0, PARTS, lambda h: reduce_c(s, (y + j) % n_y, h).start())

            loop(1, n_y + 1, send)

        @pl.when(i >= 1)
        def _():
            s = order(i - 1)

            def add(j):
                yy = (y + j) % n_y

                def one(h):
                    reduce_c(s, yy, h).wait_recv()
                    add_into(s, yy * 2 + c, h, half_of(crecv, s, yy, h))

                    @pl.when(j < n_y)
                    def _():
                        reduce_y(s, j, h).start()

                loop(0, PARTS, one)

            loop(1, n_y + 1, add)

    loop(0, n_dp + 1, produce_step)

    def reduce_step(i):
        @pl.when(i < n_dp)
        def _():
            s = order(i)

            def add(j):
                def one(h):
                    reduce_y(s, j, h).wait_recv()
                    add_into(s, me, h, half_of(yrecv, s, j, h))

                loop(0, PARTS, one)

            loop(1, n_y, add)

        @pl.when(i >= 1)
        def _():
            s = order(i - 1)

            def one(h):
                @pl.when((s >= z) & (z > 0))
                def _():
                    reduce_z(s, h, 1).wait_recv()
                    add_into(s, me, h, half_of(zrecv, 1, s, h))

                @pl.when((s <= z) & (z < n_dp - 1))
                def _():
                    reduce_z(s, h, 0).wait_recv()
                    add_into(s, me, h, half_of(zrecv, 0, s, h))

                @pl.when(s > z)
                def _():
                    reduce_z(s, h, 1).start()

                @pl.when(s < z)
                def _():
                    reduce_z(s, h, 0).start()

            loop(0, PARTS, one)

    loop(0, n_dp + 1, reduce_step)

    routed = xbuf[z, me, :, pl.ds(0, fs)].astype(F32)
    mixed = (states_ref[...].astype(F32) + routed).astype(BF16)
    mixed_ref[...] = mixed

    layer = mixed.astype(F32)
    gained = (layer * lgain_ref[...][None, :]).astype(BF16)
    out_square = jnp.sum(layer * layer, axis=1, keepdims=True)
    weight_copies[3].wait()
    pad_width = latbuf.shape[1]
    latbuf[:, pl.ds(0, lat_width)] = lax.dot_general(
        gained, wl[...], (((1,), (1,)), ((), ())), preferred_element_type=F32
    ).astype(BF16)
    high, low = split_f32(out_square)
    spare = lax.broadcasted_iota(jnp.int32, (tok, pad_width - lat_width), 1)
    latbuf[:, pl.ds(lat_width, pad_width - lat_width)] = jnp.where(
        spare == 0, high, jnp.where(spare == 1, low, 0.0)
    ).astype(BF16)

    def latent(k):
        return rem(
            latbuf, latrecv.at[k], l_send.at[k], l_recv.at[k], dp=flipped(z, k, n_dp)
        )

    for k in range(1, n_dp):
        latent(k).start()

    rope = lat_width - kvl
    turn = rope // 2
    tail = pad_width - kvl
    token = lax.broadcasted_iota(jnp.int32, (tok, tail), 0)
    across = lax.broadcasted_iota(jnp.int32, (tok, tok), 1)
    begin = jnp.int32(0)
    position = token
    owner = jnp.zeros((tok, tok), jnp.int32)
    for j in range(seqs):
        end = begin + lengths_ref[0, j]
        position = jnp.where((token >= begin) & (token < end), token - begin, position)
        owner = jnp.where((across >= begin) & (across < end), owners_ref[0, j], owner)
        begin = end
    column = lax.broadcasted_iota(jnp.int32, (tok, tail), 1)
    frequency = jnp.exp((column % turn).astype(F32) * (-2.0 * math.log(10000.0) / rope))
    angle = position.astype(F32) * frequency
    cosine = jnp.cos(angle)
    sine = jnp.sin(angle)
    sine = jnp.where(column < turn, -sine, sine)
    down = lax.broadcasted_iota(jnp.int32, (tok, tok), 0)
    mine = (owner == z).astype(F32)
    rank = jnp.dot(mine, (down < across).astype(F32), preferred_element_type=F32)
    picker = jnp.where((rank == down.astype(F32)) & (owner == z), 1.0, 0.0).astype(BF16)

    summed = latbuf[...].astype(F32)
    for k in range(1, n_dp):
        latent(k).wait_recv()
        summed += latrecv[k].astype(F32)
    end_part = summed[:, kvl:]
    in_square = jnp.where(
        (column == rope) | (column == rope + 1), end_part, 0.0
    )
    out_scale = lax.rsqrt(jnp.sum(in_square, axis=1, keepdims=True) / width + EPSILON)
    compressed = summed[:, :kvl] * out_scale
    mean_square = jnp.mean(compressed * compressed, axis=1, keepdims=True)
    normed = compressed * lax.rsqrt(mean_square + EPSILON) * kvgain_ref[...][None, :]
    keys = end_part * out_scale
    swapped = jnp.where(
        column < turn, pltpu.roll(keys, tail - turn, 1), pltpu.roll(keys, turn, 1)
    )
    rotated = keys * cosine + swapped * sine
    cache_ref[0, 0, :, pl.ds(0, kvl)] = jnp.dot(
        picker, normed.astype(BF16), preferred_element_type=F32
    ).astype(BF16)
    picked = jnp.dot(picker, rotated.astype(BF16), preferred_element_type=F32).astype(BF16)
    cache_ref[0, 0, :, pl.ds(kvl, rope)] = picked[:, :rope]

    for k in range(1, n_dp):
        latent(k).wait_send()

    def reduce_drain(s):
        def drain(h):
            @pl.when(s != z)
            def _():
                reduce_z(s, h, 1).wait_send()

            loop(1, n_y, lambda j: reduce_y(s, j, h).wait_send())
            loop(0, n_y, lambda yy: reduce_c(s, yy, h).wait_send())

        loop(0, PARTS, drain)

    loop(0, n_dp, reduce_drain)


def on_device(
    hidden_states,
    input_gain,
    expert_ids,
    route_scores,
    w_gate,
    w_up,
    w_down,
    latent_gain,
    w_latent,
    kv_gain,
    seq_lengths,
    seq_owners,
):
    tok, fs = hidden_states.shape
    n_ep = lax.axis_size("ep")
    n_dp = lax.axis_size("dp")
    n_y = n_ep // 2
    rows = n_ep * tok
    width, units = w_gate.shape[1:]
    lat_width = w_latent.shape[1]
    kvl = kv_gain.shape[0]
    pad_width = kvl + LANES
    vmem = pl.BlockSpec(memory_space=pltpu.VMEM)
    hbm = pl.BlockSpec(memory_space=pl.ANY)
    smem = pl.BlockSpec(memory_space=pltpu.SMEM)
    dma = pltpu.SemaphoreType.DMA
    return pl.pallas_call(
        functools.partial(kernel, n_ep, n_dp),
        out_shape=(
            jax.ShapeDtypeStruct((tok, fs), BF16),
            jax.ShapeDtypeStruct((1, 1, tok, lat_width), BF16),
        ),
        in_specs=[vmem, vmem, vmem, vmem, hbm, hbm, hbm, vmem, hbm, vmem, smem, smem],
        out_specs=(vmem, vmem),
        scratch_shapes=[
            pltpu.VMEM((n_dp, n_ep, tok, fs + LANES), BF16),
            pltpu.VMEM((width, units), BF16),
            pltpu.VMEM((width, units), BF16),
            pltpu.VMEM((units, width), BF16),
            pltpu.VMEM((lat_width, fs), BF16),
            pltpu.VMEM((rows, units), F32),
            pltpu.VMEM((rows, units), F32),
            pltpu.VMEM((rows, units), BF16),
            pltpu.VMEM((n_dp, n_y, tok, fs), BF16),
            pltpu.VMEM((n_dp, n_y, tok, fs), BF16),
            pltpu.VMEM((2, n_dp, tok, fs), BF16),
            pltpu.VMEM((tok, pad_width), BF16),
            pltpu.VMEM((n_dp, tok, pad_width), BF16),
            dma((4,)),
            dma((n_dp, n_ep, PARTS)),
            dma((n_dp, PARTS, 2)),
            dma((n_dp, n_y, PARTS)),
            dma((n_dp, n_y, PARTS)),
            dma((n_dp, n_y, PARTS)),
            dma((n_dp, n_y, PARTS)),
            dma((n_dp, n_y, PARTS)),
            dma((n_dp, n_y, PARTS)),
            dma((n_dp, PARTS)),
            dma((2, n_dp, PARTS)),
            dma((n_dp,)),
            dma((n_dp,)),
        ],
        compiler_params=pltpu.CompilerParams(
            collective_id=0, has_side_effects=True, vmem_limit_bytes=60 * 2**20
        ),
    )(
        hidden_states,
        input_gain,
        expert_ids.T,
        route_scores.T,
        w_gate,
        w_up,
        w_down,
        latent_gain,
        w_latent.T,
        kv_gain,
        seq_lengths,
        seq_owners,
    )


def solution(mesh):
    return jax.shard_map(
        on_device,
        mesh=mesh,
        in_specs=(
            P(("grp", "ep"), "dp"),
            P("dp"),
            P(("grp", "ep"), None),
            P(("grp", "ep"), None),
            P("ep", None, "dp"),
            P("ep", None, "dp"),
            P("ep", "dp", None),
            P("dp"),
            P("dp", None),
            P(),
            P(("grp", "ep"), None),
            P(("grp", "ep"), None),
        ),
        out_specs=(P(("grp", "ep"), "dp"), P(("grp", "ep"), "dp", None, None)),
        check_vma=False,
    )
```

```python
import functools
import math

import jax
import jax.numpy as jnp
from jax import lax
from jax.experimental import pallas as pl
from jax.experimental.pallas import tpu as pltpu
from jax.sharding import PartitionSpec as P

EPSILON = 1e-06
ROUTE_SCALE = 2.5
LANES = 128
PARTS = 2
F32 = jnp.float32
BF16 = jnp.bfloat16


def flipped(index, k, count):
    out = index
    bit = 1
    while bit < count:
        out = out + bit * ((k // bit) % 2) * (1 - 2 * ((index // bit) % 2))
        bit *= 2
    return out


def loop(lower, upper, body):
    def step(i, carry):
        body(i)
        return carry

    lax.fori_loop(lower, upper, step, 0)


def split_f32(value):
    high = value.astype(BF16).astype(F32)
    return high, value - high


def kernel(
    n_ep,
    n_dp,
    states_ref,
    gain_ref,
    ids_ref,
    scores_ref,
    wg_hbm,
    wu_hbm,
    wd_hbm,
    lgain_ref,
    wl_hbm,
    kvgain_ref,
    lengths_ref,
    owners_ref,
    mixed_ref,
    cache_ref,
    xbuf,
    wg,
    wu,
    wd,
    wl,
    acc_g,
    acc_u,
    hid,
    crecv,
    yrecv,
    zrecv,
    latbuf,
    latrecv,
    w_sem,
    g_recv,
    gz_send,
    gy_send,
    gc_send,
    rc_send,
    rc_recv,
    ry_send,
    ry_recv,
    rz_send,
    rz_recv,
    l_send,
    l_recv,
):
    tok, fs = states_ref.shape
    top = ids_ref.shape[0]
    rows = n_ep * tok
    width = fs * n_dp
    n_y = n_ep // 2
    seqs = lengths_ref.shape[1]
    kvl = kvgain_ref.shape[0]
    lat_width = wl.shape[0]
    me = lax.axis_index("ep")
    z = lax.axis_index("dp")
    y = me // 2
    c = me % 2
    peer = y * 2 + (1 - c)
    part = tok // PARTS

    def rem(src, dst, send, recv, **where):
        return pltpu.make_async_remote_copy(
            src_ref=src,
            dst_ref=dst,
            send_sem=send,
            recv_sem=recv,
            device_id=where,
            device_id_type=pl.DeviceIdType.MESH,
        )

    weight_copies = [
        pltpu.make_async_copy(wg_hbm.at[0], wg, w_sem.at[0]),
        pltpu.make_async_copy(wu_hbm.at[0], wu, w_sem.at[1]),
        pltpu.make_async_copy(wd_hbm.at[0], wd, w_sem.at[2]),
        pltpu.make_async_copy(wl_hbm, wl, w_sem.at[3]),
    ]

    barrier = pltpu.get_barrier_semaphore()
    for k in range(1, n_dp):
        pl.semaphore_signal(
            barrier, inc=1, device_id={"dp": flipped(z, k, n_dp)},
            device_id_type=pl.DeviceIdType.MESH,
        )
    for k in range(1, n_y):
        pl.semaphore_signal(
            barrier, inc=1, device_id={"ep": ((y + k) % n_y) * 2 + c},
            device_id_type=pl.DeviceIdType.MESH,
        )
    pl.semaphore_signal(
        barrier, inc=1, device_id={"ep": peer}, device_id_type=pl.DeviceIdType.MESH
    )

    states = states_ref[...].astype(F32)
    xbuf[z, me, :, pl.ds(0, fs)] = (states * gain_ref[...][None, :]).astype(BF16)
    square = jnp.sum(states * states, axis=1, keepdims=True)
    scores = scores_ref[...]
    weights = ROUTE_SCALE * scores / jnp.sum(scores, axis=0, keepdims=True)
    half = LANES // 2
    across = lax.broadcasted_iota(jnp.int32, (LANES, tok), 0) % half
    named = jnp.zeros((LANES, tok), F32)
    for k in range(top):
        named += jnp.where(across == ids_ref[k : k + 1, :], weights[k : k + 1, :], 0.0)
    lane = lax.broadcasted_iota(jnp.int32, (tok, LANES), 1)
    extra = jnp.where(lane % half == n_ep, square, named.T)
    high, low = split_f32(extra)
    xbuf[z, me, :, pl.ds(fs, LANES)] = jnp.where(lane < half, high, low).astype(BF16)

    pl.semaphore_wait(barrier, n_dp - 1 + n_y - 1 + 1)

    def block(s, b, h):
        return xbuf.at[s, b, pl.ds(pl.multiple_of(h * part, part), part)]

    def gather_z(s, h, way):
        return rem(
            block(s, me, h), block(s, me, h), gz_send.at[s, h, way], g_recv.at[s, me, h],
            dp=(z + 2 * way - 1 + n_dp) % n_dp,
        )

    def relay(s, h, act):
        @pl.when((s <= z) & (z + 1 < n_dp))
        def _():
            act(gather_z(s, h, 1))

        @pl.when((s >= z) & (z > 0))
        def _():
            act(gather_z(s, h, 0))

    def gather_y(s, j, h):
        to = ((y + j) % n_y) * 2 + c
        return rem(
            block(s, me, h), block(s, me, h), gy_send.at[s, j, h], g_recv.at[s, me, h], ep=to
        )

    def gather_c(s, yy, h):
        b = yy * 2 + c
        return rem(
            block(s, b, h), block(s, b, h), gc_send.at[s, yy, h], g_recv.at[s, b, h], ep=peer
        )

    def gather_wait(s, b, h):
        rem(
            block(s, b, h), block(s, b, h), g_recv.at[s, b, h], g_recv.at[s, b, h], ep=peer
        ).wait_recv()

    def at_distance(i, body):
        @pl.when(z - i >= 0)
        def _():
            body(z - i)

        @pl.when((i > 0) & (z + i < n_dp))
        def _():
            body(z + i)

    acc_g[...] = jnp.zeros_like(acc_g)
    acc_u[...] = jnp.zeros_like(acc_u)

    def spread(i):
        def body(s):
            def send(h):
                @pl.when(i > 0)
                def _():
                    gather_wait(s, me, h)

                relay(s, h, lambda copy: copy.start())
                loop(1, n_y, lambda j: gather_y(s, j, h).start())
                gather_c(s, y, h).start()

            loop(0, PARTS, send)

        at_distance(i, body)

    def across_core(s):
        def forward(j):
            yy = (y + j) % n_y

            def send(h):
                gather_wait(s, yy * 2 + c, h)
                gather_c(s, yy, h).start()

            loop(0, PARTS, send)

        loop(1, n_y, forward)

    def multiply(s):
        def arrive(yy):
            loop(0, PARTS, lambda h: gather_wait(s, yy * 2 + (1 - c), h))

        loop(0, n_y, arrive)
        slab = xbuf[s, :, :, pl.ds(0, fs)].reshape(rows, fs)
        depth = pl.ds(pl.multiple_of(s * fs, LANES), fs)
        acc_g[...] += jnp.dot(slab, wg[depth, :], preferred_element_type=F32)
        acc_u[...] += jnp.dot(slab, wu[depth, :], preferred_element_type=F32)

    def gather_step(i):
        @pl.when(i < n_dp)
        def _():
            spread(i)

        @pl.when(i == 0)
        def _():
            for copy in weight_copies:
                copy.start()

        @pl.when(i == 2)
        def _():
            weight_copies[0].wait()
            weight_copies[1].wait()

        @pl.when(i >= 2)
        def _():
            at_distance(i - 2, multiply)

        @pl.when((i >= 1) & (i <= n_dp))
        def _():
            at_distance(i - 1, across_core)

    loop(0, n_dp + 2, gather_step)

    side = jnp.zeros((rows, LANES), F32)
    wide_lane = lax.broadcasted_iota(jnp.int32, (rows, LANES), 1) % half
    for s in range(n_dp):
        lanes = xbuf[s, :, :, pl.ds(fs, LANES)].reshape(rows, LANES).astype(F32)
        if s == 0:
            route = jnp.sum(jnp.where(wide_lane == me, lanes, 0.0), axis=1, keepdims=True)
        side += lanes
    total = jnp.sum(jnp.where(wide_lane == n_ep, side, 0.0), axis=1, keepdims=True)
    scale = lax.rsqrt(total / width + EPSILON)
    gate = acc_g[...] * scale
    up = acc_u[...] * scale
    hid[...] = (route * (gate / (1.0 + jnp.exp(-gate)) * up)).astype(BF16)

    def gather_drain(s):
        def drain(h):
            relay(s, h, lambda copy: copy.wait_send())
            loop(1, n_y, lambda j: gather_y(s, j, h).wait_send())
            loop(0, n_y, lambda yy: gather_c(s, yy, h).wait_send())

        loop(0, PARTS, drain)

    loop(0, n_dp, gather_drain)
    weight_copies[2].wait()

    def slot(s, b, h):
        return xbuf.at[s, b, pl.ds(pl.multiple_of(h * part, part), part), pl.ds(0, fs)]

    def half_of(buf, s, j, h):
        return buf.at[s, j, pl.ds(pl.multiple_of(h * part, part), part)]

    def reduce_c(s, yy, h):
        return rem(
            slot(s, yy * 2 + (1 - c), h), half_of(crecv, s, yy, h),
            rc_send.at[s, yy, h], rc_recv.at[s, yy, h], ep=peer,
        )

    def reduce_y(s, j, h):
        to = (y + j) % n_y
        return rem(
            slot(s, to * 2 + c, h), half_of(yrecv, s, j, h),
            ry_send.at[s, j, h], ry_recv.at[s, j, h], ep=to * 2 + c,
        )

    def reduce_z(s, h, way):
        return rem(
            slot(s, me, h), half_of(zrecv, way, s, h),
            rz_send.at[s, h], rz_recv.at[way, s, h], dp=(z + 2 * way - 1 + n_dp) % n_dp,
        )

    def add_into(s, b, h, arrived):
        here = slot(s, b, h)
        here[...] = (here[...].astype(F32) + arrived[...].astype(F32)).astype(BF16)

    def order(q):
        ahead = n_dp - 1 - z
        low = jnp.where(q < ahead, n_dp - 1 - q, q - ahead)
        high = jnp.where(q < z, q, n_dp - 1 - (q - z))
        return jnp.where(q == n_dp - 1, z, jnp.where(2 * z < n_dp, low, high))

    tile = 256 if fs % 256 == 0 else LANES

    def produce_step(i):
        @pl.when(i < n_dp)
        def _():
            s = order(i)
            for n in range(fs // tile):
                cols = pl.ds(pl.multiple_of(s * fs + n * tile, LANES), tile)
                out = jnp.dot(hid[...], wd[:, cols], preferred_element_type=F32)
                xbuf[s, :, :, pl.ds(n * tile, tile)] = out.astype(BF16).reshape(n_ep, tok, tile)

            def send(j):
                loop(0, PARTS, lambda h: reduce_c(s, (y + j) % n_y, h).start())

            loop(1, n_y + 1, send)

        @pl.when(i >= 1)
        def _():
            s = order(i - 1)

            def add(j):
                yy = (y + j) % n_y

                def one(h):
                    reduce_c(s, yy, h).wait_recv()
                    add_into(s, yy * 2 + c, h, half_of(crecv, s, yy, h))

                    @pl.when(j < n_y)
                    def _():
                        reduce_y(s, j, h).start()

                loop(0, PARTS, one)

            loop(1, n_y + 1, add)

    loop(0, n_dp + 1, produce_step)

    def reduce_step(i):
        @pl.when(i < n_dp)
        def _():
            s = order(i)

            def add(j):
                def one(h):
                    reduce_y(s, j, h).wait_recv()
                    add_into(s, me, h, half_of(yrecv, s, j, h))

                loop(0, PARTS, one)

            loop(1, n_y, add)

        @pl.when(i >= 1)
        def _():
            s = order(i - 1)

            def one(h):
                @pl.when((s >= z) & (z > 0))
                def _():
                    reduce_z(s, h, 1).wait_recv()
                    add_into(s, me, h, half_of(zrecv, 1, s, h))

                @pl.when((s <= z) & (z < n_dp - 1))
                def _():
                    reduce_z(s, h, 0).wait_recv()
                    add_into(s, me, h, half_of(zrecv, 0, s, h))

                @pl.when(s > z)
                def _():
                    reduce_z(s, h, 1).start()

                @pl.when(s < z)
                def _():
                    reduce_z(s, h, 0).start()

            loop(0, PARTS, one)

    loop(0, n_dp + 1, reduce_step)

    routed = xbuf[z, me, :, pl.ds(0, fs)].astype(F32)
    mixed = (states_ref[...].astype(F32) + routed).astype(BF16)
    mixed_ref[...] = mixed

    layer = mixed.astype(F32)
    gained = (layer * lgain_ref[...][None, :]).astype(BF16)
    out_square = jnp.sum(layer * layer, axis=1, keepdims=True)
    weight_copies[3].wait()
    pad_width = latbuf.shape[1]
    latbuf[:, pl.ds(0, lat_width)] = lax.dot_general(
        gained, wl[...], (((1,), (1,)), ((), ())), preferred_element_type=F32
    ).astype(BF16)
    high, low = split_f32(out_square)
    spare = lax.broadcasted_iota(jnp.int32, (tok, pad_width - lat_width), 1)
    latbuf[:, pl.ds(lat_width, pad_width - lat_width)] = jnp.where(
        spare == 0, high, jnp.where(spare == 1, low, 0.0)
    ).astype(BF16)

    def latent(k):
        return rem(
            latbuf, latrecv.at[k], l_send.at[k], l_recv.at[k], dp=flipped(z, k, n_dp)
        )

    for k in range(1, n_dp):
        latent(k).start()

    rope = lat_width - kvl
    turn = rope // 2
    tail = pad_width - kvl
    token = lax.broadcasted_iota(jnp.int32, (tok, tail), 0)
    across = lax.broadcasted_iota(jnp.int32, (tok, tok), 1)
    begin = jnp.int32(0)
    position = token
    owner = jnp.zeros((tok, tok), jnp.int32)
    for j in range(seqs):
        end = begin + lengths_ref[0, j]
        position = jnp.where((token >= begin) & (token < end), token - begin, position)
        owner = jnp.where((across >= begin) & (across < end), owners_ref[0, j], owner)
        begin = end
    column = lax.broadcasted_iota(jnp.int32, (tok, tail), 1)
    frequency = jnp.exp((column % turn).astype(F32) * (-2.0 * math.log(10000.0) / rope))
    angle = position.astype(F32) * frequency
    cosine = jnp.cos(angle)
    sine = jnp.sin(angle)
    sine = jnp.where(column < turn, -sine, sine)
    down = lax.broadcasted_iota(jnp.int32, (tok, tok), 0)
    mine = (owner == z).astype(F32)
    rank = jnp.dot(mine, (down < across).astype(F32), preferred_element_type=F32)
    picker = jnp.where((rank == down.astype(F32)) & (owner == z), 1.0, 0.0).astype(BF16)

    summed = latbuf[...].astype(F32)
    for k in range(1, n_dp):
        latent(k).wait_recv()
        summed += latrecv[k].astype(F32)
    end_part = summed[:, kvl:]
    in_square = jnp.where(
        (column == rope) | (column == rope + 1), end_part, 0.0
    )
    out_scale = lax.rsqrt(jnp.sum(in_square, axis=1, keepdims=True) / width + EPSILON)
    compressed = summed[:, :kvl] * out_scale
    mean_square = jnp.mean(compressed * compressed, axis=1, keepdims=True)
    normed = compressed * lax.rsqrt(mean_square + EPSILON) * kvgain_ref[...][None, :]
    keys = end_part * out_scale
    swapped = jnp.where(
        column < turn, pltpu.roll(keys, tail - turn, 1), pltpu.roll(keys, turn, 1)
    )
    rotated = keys * cosine + swapped * sine
    cache_ref[0, 0, :, pl.ds(0, kvl)] = jnp.dot(
        picker, normed.astype(BF16), preferred_element_type=F32
    ).astype(BF16)
    picked = jnp.dot(picker, rotated.astype(BF16), preferred_element_type=F32).astype(BF16)
    cache_ref[0, 0, :, pl.ds(kvl, rope)] = picked[:, :rope]

    for k in range(1, n_dp):
        latent(k).wait_send()

    def reduce_drain(s):
        def drain(h):
            @pl.when(s != z)
            def _():
                reduce_z(s, h, 1).wait_send()

            loop(1, n_y, lambda j: reduce_y(s, j, h).wait_send())
            loop(0, n_y, lambda yy: reduce_c(s, yy, h).wait_send())

        loop(0, PARTS, drain)

    loop(0, n_dp, reduce_drain)


def on_device(
    hidden_states,
    input_gain,
    expert_ids,
    route_scores,
    w_gate,
    w_up,
    w_down,
    latent_gain,
    w_latent,
    kv_gain,
    seq_lengths,
    seq_owners,
):
    tok, fs = hidden_states.shape
    n_ep = lax.axis_size("ep")
    n_dp = lax.axis_size("dp")
    n_y = n_ep // 2
    rows = n_ep * tok
    width, units = w_gate.shape[1:]
    lat_width = w_latent.shape[1]
    kvl = kv_gain.shape[0]
    pad_width = kvl + LANES
    vmem = pl.BlockSpec(memory_space=pltpu.VMEM)
    hbm = pl.BlockSpec(memory_space=pl.ANY)
    smem = pl.BlockSpec(memory_space=pltpu.SMEM)
    dma = pltpu.SemaphoreType.DMA
    return pl.pallas_call(
        functools.partial(kernel, n_ep, n_dp),
        out_shape=(
            jax.ShapeDtypeStruct((tok, fs), BF16),
            jax.ShapeDtypeStruct((1, 1, tok, lat_width), BF16),
        ),
        in_specs=[vmem, vmem, vmem, vmem, hbm, hbm, hbm, vmem, hbm, vmem, smem, smem],
        out_specs=(vmem, vmem),
        scratch_shapes=[
            pltpu.VMEM((n_dp, n_ep, tok, fs + LANES), BF16),
            pltpu.VMEM((width, units), BF16),
            pltpu.VMEM((width, units), BF16),
            pltpu.VMEM((units, width), BF16),
            pltpu.VMEM((lat_width, fs), BF16),
            pltpu.VMEM((rows, units), F32),
            pltpu.VMEM((rows, units), F32),
            pltpu.VMEM((rows, units), BF16),
            pltpu.VMEM((n_dp, n_y, tok, fs), BF16),
            pltpu.VMEM((n_dp, n_y, tok, fs), BF16),
            pltpu.VMEM((2, n_dp, tok, fs), BF16),
            pltpu.VMEM((tok, pad_width), BF16),
            pltpu.VMEM((n_dp, tok, pad_width), BF16),
            dma((4,)),
            dma((n_dp, n_ep, PARTS)),
            dma((n_dp, PARTS, 2)),
            dma((n_dp, n_y, PARTS)),
            dma((n_dp, n_y, PARTS)),
            dma((n_dp, n_y, PARTS)),
            dma((n_dp, n_y, PARTS)),
            dma((n_dp, n_y, PARTS)),
            dma((n_dp, n_y, PARTS)),
            dma((n_dp, PARTS)),
            dma((2, n_dp, PARTS)),
            dma((n_dp,)),
            dma((n_dp,)),
        ],
        compiler_params=pltpu.CompilerParams(
            collective_id=0, has_side_effects=True, vmem_limit_bytes=60 * 2**20
        ),
    )(
        hidden_states,
        input_gain,
        expert_ids.T,
        route_scores.T,
        w_gate,
        w_up,
        w_down,
        latent_gain,
        w_latent.T,
        kv_gain,
        seq_lengths,
        seq_owners,
    )


def solution(mesh):
    return jax.shard_map(
        on_device,
        mesh=mesh,
        in_specs=(
            P(("grp", "ep"), "dp"),
            P("dp"),
            P(("grp", "ep"), None),
            P(("grp", "ep"), None),
            P("ep", None, "dp"),
            P("ep", None, "dp"),
            P("ep", "dp", None),
            P("dp"),
            P("dp", None),
            P(),
            P(("grp", "ep"), None),
            P(("grp", "ep"), None),
        ),
        out_specs=(P(("grp", "ep"), "dp"), P(("grp", "ep"), "dp", None, None)),
        check_vma=False,
    )
```
